1024 devices in a mesh: row: 8 (over z_lo), col: 128 (over y, x, z_hi, core).
Axes of the slice: x: 4, y: 8, z: 16 (z_hi: 2, z_lo: 8; z = z_hi * 8 + z_lo), core: 2. Of those that a mesh axis runs over, the one named last changes fastest.
Arguments:
- kernel: bfloat16 [2, 2, 32768, 2048], P(None, None, 'col', 'row'), may hold values from -0.0234375 to 0.0234375
- probes: bfloat16 [256, 2, 2, 32768], P(None, None, None, 'col'), may hold values from -6 to 6
- noise_var: float32 [2, 32768], P(None, 'col'), may hold values from 0.05 to 0.5
- prior_diag: float32 [2048], P('row'), may hold values from 2.2 to 4
Outputs:
- hess_probes: float32 [256, 2, 2, 32768], P('row', None, None, 'col')
The draws below stay inside these ranges and needn't reach their ends.
All inputs are finite; a program needn't handle non-finite values.
Results may differ from the reference program's by a relative error of at most 0.015.
Values may be sent and summed in bfloat16 or wider, within the bound.
A program may use at most 32 MiB of HBM per device.

```python
import math
import jax
import jax.numpy as jnp

NF = 2
P_DEV = 256
NCOL = 256
NP = 2048
NR = 32768
N_ROW = 8


def block_levels(stream_key, shape, cuts, smallest, top_value):
    def one(axis_at, blocks):
        heights = jax.random.uniform(jax.random.fold_in(jax.random.fold_in(stream_key, 6), axis_at), (blocks,), jnp.float32, smallest / len(cuts), top_value / len(cuts))
        return jnp.repeat(jnp.exp(heights), shape[axis_at] // blocks).reshape((-1,) + (1,) * (len(shape) - axis_at - 1))

    level = one(*cuts[0])
    for cut in cuts[1:]:
        level = level * one(*cut)
    return level


def noise(stream_key, dims, scale, bound, split=(), dtype=jnp.bfloat16):
    array = jax.random.normal(stream_key, dims, jnp.float32) * scale
    if len(split) > 0:
        array = block_levels(stream_key, dims, split, -0.22, 0.18) * array
    return jnp.clip(array, min=-bound, max=bound).astype(dtype)


def setup_inputs(seed: int = 0) -> dict:
    seeds = jax.random.split(jax.random.key(seed), 5)
    return {
        "kernel": noise(seeds[0], (NF, 2, NR, NP), (2 * NR) ** -0.5, 0.0234375, ((2, 128), (3, 8))),
        "probes": noise(seeds[1], (NCOL, NF, 2, NR), 1.0, 6.0, ((3, 128),)),
        "noise_var": jnp.clip(jnp.exp(math.log(0.5) - 2.3025851 * jax.random.uniform(seeds[2], (NF, NR), jnp.float32) ** block_levels(seeds[2], (NF, NR), ((1, 128),), -0.2, 0.2)), 0.05, 0.5),
        "prior_diag": jnp.clip(2.2 + 1.8 * jax.random.uniform(seeds[3], (NP,), jnp.float32) ** block_levels(seeds[3], (NP,), ((0, 8),), -0.2, 0.2), 2.2, 4.0),
    }


def sweep(field, coef):
    padded = jnp.pad(field, ((0, 0), (1, 1)))
    return coef * field - padded[:, :-2] - padded[:, 2:]


def reference(kernel, probes, noise_var, prior_diag):
    adjoint = []
    for freq_no in range(NF):
        real_part = probes[:, freq_no, 0, :]
        imag_part = probes[:, freq_no, 1, :]
        upper = jnp.concatenate([real_part, imag_part], axis=1)
        lower = jnp.concatenate([imag_part, -real_part], axis=1)
        stacked = kernel[freq_no].reshape(2 * NR, NP)
        adjoint.append(jnp.dot(jnp.concatenate([upper, lower], axis=0), stacked, preferred_element_type=jnp.float32))
    adjoint = jnp.stack(adjoint).reshape(NF * 2 * NCOL, NP)
    smooth = sweep(sweep(adjoint, prior_diag), prior_diag)
    smooth = smooth.astype(jnp.bfloat16).reshape(NF, 2, NCOL, NP)
    total = jnp.zeros((NCOL, NF, 2, NR), jnp.float32)
    for block in range(N_ROW):
        low = block * P_DEV
        parts = []
        for freq_no in range(NF):
            field = jnp.concatenate([smooth[freq_no, 0, :, low:low + P_DEV], smooth[freq_no, 1, :, low:low + P_DEV]], axis=0)
            stacked = kernel[freq_no, :, :, low:low + P_DEV].reshape(2 * NR, P_DEV)
            prod = jax.lax.dot_general(field, stacked, (((1,), (1,)), ((), ())), preferred_element_type=jnp.float32)
            real_out = prod[:NCOL, :NR] - prod[NCOL:, NR:]
            imag_out = prod[NCOL:, :NR] + prod[:NCOL, NR:]
            parts.append(jnp.stack([real_out, imag_out], axis=1))
        partial_value = jnp.stack(parts, axis=1).astype(jnp.bfloat16)
        total = total + partial_value.astype(jnp.float32)
    return total + noise_var[None, :, None, :] * probes.astype(jnp.float32)
```

```python
import functools

import jax
import jax.numpy as jnp
from jax import lax
from jax.experimental import pallas as pl
from jax.experimental.pallas import tpu as pltpu
from jax.sharding import PartitionSpec as P

F32 = jnp.float32
BF16 = jnp.bfloat16
MESH = pl.DeviceIdType.MESH


def nt(a, b):
    return lax.dot_general(a, b, (((1,), (1,)), ((), ())), preferred_element_type=F32)


def nn(a, b):
    return jnp.dot(a, b, preferred_element_type=F32)


def body(
    n_row, n_col,
    k_hbm, v_hbm, nv_ref, d_ref, o_ref,
    kv, vv, kh, dsend, dh, kp, s0, r0, ao, s1, r1, zs, zr, fc, g, hs, r2, l2s, r3,
    load_sem, halo_s, halo_r, core_s, core_r, rs_s, rs_r, z_s, z_r, ag_s, ag_r, cag_s, cag_r,
    h_s, h_r, l2_sem, l2_r,
):
    row = lax.axis_index("row")
    col = lax.axis_index("col")
    n_xy = n_col // 4
    n_j = n_row // 2
    core = lax.rem(col, 2)
    zh = lax.rem(lax.div(col, 2), 2)
    cxy = lax.div(col, 4)
    half = lax.div(row, n_j)
    j = lax.rem(row, n_j)
    n_cb = 512 // n_xy
    pw = 256 // n_row
    other = 1 - core

    sib = (row, cxy * 4 + zh * 2 + other)
    zpart = (row, cxy * 4 + (1 - zh) * 2 + core)

    def xy_dev(k):
        t = lax.rem(cxy + k, n_xy)
        return t, (row, t * 4 + zh * 2 + core)

    def remote(src, dst, ss, rs, dev):
        return pltpu.make_async_remote_copy(
            src_ref=src, dst_ref=dst, send_sem=ss, recv_sem=rs, device_id=dev, device_id_type=MESH
        )

    barrier = pltpu.get_barrier_semaphore()

    def signal(dev):
        pl.semaphore_signal(barrier, inc=1, device_id=dev, device_id_type=MESH)

    load_k = pltpu.make_async_copy(k_hbm, kv, load_sem.at[0])
    load_v = pltpu.make_async_copy(v_hbm, vv, load_sem.at[1])
    load_k.start()
    load_v.start()
    signal(zpart)
    signal(sib)

    def sig_xy(k, c):
        signal(xy_dev(k)[1])
        return c

    lax.fori_loop(1, n_xy, sig_xy, 0)

    def sig_row(k, c):
        signal((lax.rem(row + k, n_row), col))
        return c

    lax.fori_loop(1, n_row, sig_row, 0)

    dsend[0] = jnp.broadcast_to(d_ref[:, 128:256], (8, 128))
    dsend[1] = jnp.broadcast_to(d_ref[:, 0:128], (8, 128))
    load_k.wait()
    load_v.wait()

    def adjoint(f):
        base = pl.multiple_of(f * 512, 512)
        vr = vv[pl.ds(base, 256), :]
        vi = vv[pl.ds(base + 256, 256), :]
        kr = kv[pl.ds(base, 256), :]
        ki = kv[pl.ds(base + 256, 256), :]
        return nn(vr, kr) + nn(vi, ki), nn(vi, kr) - nn(vr, ki)

    re, im = adjoint(other)
    s0[0:256, :] = re.astype(BF16)
    s0[256:512, :] = im.astype(BF16)
    pl.semaphore_wait(barrier, n_xy - 1 + n_row - 1 + 2)
    core_rs = remote(s0, r0, core_s, core_r, sib)
    core_rs.start()
    re, im = adjoint(core)
    ao[0:256, :] = re
    ao[256:512, :] = im

    up_dev = (jnp.minimum(row + 1, n_row - 1), col)
    down_dev = (jnp.maximum(row - 1, 0), col)
    up = [
        remote(kv.at[:, pl.ds(128, 128)], kh.at[0], halo_s.at[0], halo_r.at[0], up_dev),
        remote(dsend.at[0], dh.at[0], halo_s.at[1], halo_r.at[1], up_dev),
    ]
    down = [
        remote(kv.at[:, pl.ds(0, 128)], kh.at[1], halo_s.at[2], halo_r.at[2], down_dev),
        remote(dsend.at[1], dh.at[1], halo_s.at[3], halo_r.at[3], down_dev),
    ]

    @pl.when(row < n_row - 1)
    def _():
        for cp in up:
            cp.start()

    @pl.when(row > 0)
    def _():
        for cp in down:
            cp.start()

    core_rs.wait_recv()
    s1[...] = (ao[...] + r0[...].astype(F32)).astype(BF16)

    def chunk(t):
        return pl.ds(pl.multiple_of(t * n_cb, n_cb), n_cb)

    def rs_copy(k):
        t, dev = xy_dev(k)
        return remote(s1.at[chunk(t)], r1.at[chunk(cxy)], rs_s, rs_r, dev)

    def rs_start(k, c):
        rs_copy(k).start()
        return c

    lax.fori_loop(1, n_xy, rs_start, 0)
    r1[chunk(cxy), :] = s1[chunk(cxy), :]

    @pl.when(row > 0)
    def _():
        remote(kv.at[:, pl.ds(128, 128)], kh.at[0], halo_s.at[0], halo_r.at[0], up_dev).wait_recv()
        remote(dsend.at[0], dh.at[0], halo_s.at[1], halo_r.at[1], up_dev).wait_recv()

    @pl.when(row < n_row - 1)
    def _():
        remote(kv.at[:, pl.ds(0, 128)], kh.at[1], halo_s.at[2], halo_r.at[2], down_dev).wait_recv()
        remote(dsend.at[1], dh.at[1], halo_s.at[3], halo_r.at[3], down_dev).wait_recv()

    @pl.when(row == 0)
    def _():
        kh[0] = jnp.zeros((1024, 128), BF16)
        dh[0] = jnp.zeros((8, 128), F32)

    @pl.when(row == n_row - 1)
    def _():
        kh[1] = jnp.zeros((1024, 128), BF16)
        dh[1] = jnp.zeros((8, 128), F32)

    coef = jnp.concatenate([dh[0, 0:1, :], d_ref[...], dh[1, 0:1, :]], axis=1)
    lane = lax.broadcasted_iota(jnp.int32, (1, 512), 1)
    low = jnp.where(row > 0, 0, 128)
    high = jnp.where(row < n_row - 1, 512, 384)
    inside = jnp.where((lane >= low) & (lane < high), 1.0, 0.0).astype(F32)

    def stencil(i, c):
        rows = pl.ds(pl.multiple_of(i * 32, 32), 32)
        e = jnp.concatenate([kh[0, rows, :], kv[rows, :], kh[1, rows, :]], axis=1).astype(F32)
        for _ in range(2):
            e = inside * (coef * e - pltpu.roll(e, 1, 1) - pltpu.roll(e, 511, 1))
        kp[rows, :] = e[:, 128:384].astype(BF16)
        return c

    lax.fori_loop(0, 32, stencil, 0)

    span = pl.ds(0, (n_xy - 1) * n_cb)
    remote(r1.at[span], r1.at[span], rs_s, rs_r, sib).wait_recv()
    acc = r1[0:n_cb, :].astype(F32)
    for s in range(1, n_xy):
        acc = acc + r1[s * n_cb:(s + 1) * n_cb, :].astype(F32)

    zs[...] = acc.astype(BF16)
    z_copy = remote(zs, zr, z_s, z_r, zpart)
    z_copy.start()
    z_copy.wait_recv()
    final = (acc + zr[...].astype(F32)).astype(BF16)
    fc[...] = final

    def ag_copy(k):
        _, dev = xy_dev(k)
        return remote(fc, g.at[core, chunk(cxy)], ag_s, ag_r, dev)

    def ag_start(k, c):
        ag_copy(k).start()
        return c

    lax.fori_loop(1, n_xy, ag_start, 0)
    g[core, chunk(cxy), :] = final
    remote(r1.at[span], g.at[core, span], ag_s, ag_r, sib).wait_recv()
    cag = remote(g.at[core], g.at[core], cag_s, cag_r, sib)
    cag.start()

    def row_dev(jt):
        return (half * n_j + jt, col)

    def forward(f):
        base = pl.multiple_of(f * 512, 512)
        kr = kp[pl.ds(base, 256), :]
        ki = kp[pl.ds(base + 256, 256), :]
        for q in (1 - half, half):
            first = pl.multiple_of(q * 128, 128)
            ar = g[f, pl.ds(first, 128), :]
            ai = g[f, pl.ds(first + 256, 128), :]
            hr = (nt(ar, kr) - nt(ai, ki)).astype(BF16)
            hi = (nt(ar, ki) + nt(ai, kr)).astype(BF16)
            for jj in range(n_j):
                hs[q, f, jj, 0:pw, :] = hr[jj * pw:(jj + 1) * pw, :]
                hs[q, f, jj, pw:2 * pw, :] = hi[jj * pw:(jj + 1) * pw, :]

            for k in range(1, n_j):
                jt = lax.rem(j + k, n_j)
                remote(
                    hs.at[q, f, jt], r2.at[q, f, k - 1], h_s.at[q, f], h_r.at[q, f], row_dev(jt)
                ).start()

    def half_sum(q, f):
        remote(r2.at[q, f], r2.at[q, f], h_s.at[q, f], h_r.at[q, f], sib).wait_recv()
        total = hs[q, f, j].astype(F32)
        for k in range(n_j - 1):
            total = total + r2[q, f, k].astype(F32)
        return total

    def across(f):
        return remote(l2s.at[f], r3.at[f], l2_sem.at[f], l2_r.at[f], ((1 - half) * n_j + j, col))

    forward(core)
    remote(g.at[other], g.at[other], cag_s, cag_r, sib).wait_recv()
    forward(other)
    for f in (core, other):
        l2s[f] = half_sum(1 - half, f).astype(BF16)
        across(f).start()
    for f in (core, other):
        total = half_sum(half, f)
        across(f).wait_recv()
        total = total + r3[f].astype(F32)
        level = nv_ref[pl.ds(f, 1), :]
        for c in range(2):
            own = vv[pl.ds(pl.multiple_of(f * 512 + c * 256 + row * pw, pw), pw), :].astype(F32)
            o_ref[pl.ds(pl.multiple_of((f * 2 + c) * pw, pw), pw), :] = (
                total[c * pw:(c + 1) * pw, :] + level * own
            )

    core_rs.wait_send()

    @pl.when(row < n_row - 1)
    def _():
        for cp in up:
            cp.wait_send()

    @pl.when(row > 0)
    def _():
        for cp in down:
            cp.wait_send()

    remote(r1.at[span], r1.at[span], rs_s, rs_r, sib).wait_send()
    z_copy.wait_send()
    remote(r1.at[span], r1.at[span], ag_s, ag_r, sib).wait_send()
    cag.wait_send()
    for f in range(2):
        for q in range(2):
            remote(r2.at[q, f], r2.at[q, f], h_s.at[q, f], h_r.at[q, f], sib).wait_send()
        across(f).wait_send()


def shards(kernel, probes, noise_var, prior_diag):
    n_row = lax.axis_size("row")
    n_col = lax.axis_size("col")
    n_j = n_row // 2
    pw = 256 // n_row
    n_cb = 512 // (n_col // 4)
    v = jnp.transpose(probes, (1, 2, 0, 3)).reshape(1024, 256)
    k = kernel.reshape(1024, 256)
    vmem = pl.BlockSpec(memory_space=pltpu.VMEM)
    hbm = pl.BlockSpec(memory_space=pl.ANY)
    dma = pltpu.SemaphoreType.DMA
    out = pl.pallas_call(
        functools.partial(body, n_row, n_col),
        out_shape=jax.ShapeDtypeStruct((4 * pw, 256), F32),
        in_specs=[hbm, hbm, vmem, vmem],
        out_specs=vmem,
        scratch_shapes=[
            pltpu.VMEM((1024, 256), BF16),
            pltpu.VMEM((1024, 256), BF16),
            pltpu.VMEM((2, 1024, 128), BF16),
            pltpu.VMEM((2, 8, 128), F32),
            pltpu.VMEM((2, 8, 128), F32),
            pltpu.VMEM((1024, 256), BF16),
            pltpu.VMEM((512, 256), BF16),
            pltpu.VMEM((512, 256), BF16),
            pltpu.VMEM((512, 256), F32),
            pltpu.VMEM((512, 256), BF16),
            pltpu.VMEM((512, 256), BF16),
            pltpu.VMEM((n_cb, 256), BF16),
            pltpu.VMEM((n_cb, 256), BF16),
            pltpu.VMEM((n_cb, 256), BF16),
            pltpu.VMEM((2, 512, 256), BF16),
            pltpu.VMEM((2, 2, n_j, 2 * pw, 256), BF16),
            pltpu.VMEM((2, 2, n_j - 1, 2 * pw, 256), BF16),
            pltpu.VMEM((2, 2 * pw, 256), BF16),
            pltpu.VMEM((2, 2 * pw, 256), BF16),
            dma((2,)), dma((4,)), dma((4,)), dma, dma, dma, dma, dma, dma, dma, dma, dma, dma,
            dma((2, 2)), dma((2, 2)), dma((2,)), dma((2,)),
        ],
        compiler_params=pltpu.CompilerParams(
            collective_id=0, has_side_effects=True, vmem_limit_bytes=32 * 1024 * 1024
        ),
    )(k, v, noise_var, prior_diag.reshape(1, 256))
    return jnp.transpose(out.reshape(2, 2, pw, 256), (2, 0, 1, 3))


def solution(mesh):
    in_specs = (P(None, None, "col", "row"), P(None, None, None, "col"), P(None, "col"), P("row"))
    out_specs = P("row", None, None, "col")
    return jax.shard_map(shards, mesh=mesh, in_specs=in_specs, out_specs=out_specs, check_vma=False)
```

```python
import functools

import jax
import jax.numpy as jnp
from jax import lax
from jax.experimental import pallas as pl
from jax.experimental.pallas import tpu as pltpu
from jax.sharding import PartitionSpec as P

F32 = jnp.float32
BF16 = jnp.bfloat16
MESH = pl.DeviceIdType.MESH


def nt(a, b):
    return lax.dot_general(a, b, (((1,), (1,)), ((), ())), preferred_element_type=F32)


def nn(a, b):
    return jnp.dot(a, b, preferred_element_type=F32)


def body(
    n_row, n_col,
    k_hbm, v_hbm, nv_hbm, d_hbm, o_ref,
    kv, vraw, vv, nv_ref, d_ref, kh, dsend, dh, kp, s0, r0, ao, s1, r1, zs, zr, fc, g, hs, r2, rg, l2s, rc,
    load_sem, halo_s, halo_r, core_s, core_r, rs_s, rs_r, z_s, z_r, ag_s, ag_r, cag_s, cag_r,
    kx_s, kx_r, h_s, h_r, g_s, g_r, cr_s, cr_r,
):
    row = lax.axis_index("row")
    col = lax.axis_index("col")
    n_xy = n_col // 4
    n_j = n_row // 2
    core = lax.rem(col, 2)
    zh = lax.rem(lax.div(col, 2), 2)
    cxy = lax.div(col, 4)
    half = lax.div(row, n_j)
    j = lax.rem(row, n_j)
    a = lax.div(j, 2)
    b = lax.rem(j, 2)
    n_cb = 512 // n_xy
    pw = 256 // n_row
    other = 1 - core
    batches = (0, 1)

    sib = (row, cxy * 4 + zh * 2 + other)
    pair_row = row + 1 - 2 * b
    pair = (pair_row, col)
    zcol = cxy * 4 + (1 - zh) * 2 + core
    zpart = (row, zcol)
    zpair = (pair_row, zcol)
    mate = (half * n_j + (1 - a) * 2 + b, col)
    beyond = ((1 - half) * n_j + j, col)

    def xy_dev(i):
        step = lax.div(i + 1, 2)
        k = n_xy // 2 + jnp.where(lax.rem(i, 2) == 1, -step, step)
        t = lax.rem(cxy + k, n_xy)
        return t, (row, t * 4 + zh * 2 + core)

    def remote(src, dst, ss, rs, dev):
        return pltpu.make_async_remote_copy(
            src_ref=src, dst_ref=dst, send_sem=ss, recv_sem=rs, device_id=dev, device_id_type=MESH
        )

    barrier = pltpu.get_barrier_semaphore()

    def signal(dev):
        pl.semaphore_signal(barrier, inc=1, device_id=dev, device_id_type=MESH)

    def sig_xy(i, c):
        signal(xy_dev(i)[1])
        return c

    lax.fori_loop(0, n_xy - 1, sig_xy, 0)
    signal(beyond)
    signal(mate)
    signal(pair)
    signal(sib)
    inland = (row > 0) & (row < n_row - 1)

    @pl.when(inland)
    def _():
        signal((row - 1 + 2 * b, col))

    loads = [
        pltpu.make_async_copy(src, dst, load_sem.at[i])
        for i, (src, dst) in enumerate(
            ((v_hbm, vraw), (k_hbm, kv), (d_hbm, d_ref), (nv_hbm, nv_ref))
        )
    ]
    for cp in loads:
        cp.start()

    loads[0].wait()

    def order(i, c):
        for f in range(2):
            x = jnp.swapaxes(vraw[pl.ds(i * 2 * pw, 2 * pw), f].astype(F32), 0, 1)
            x = jnp.swapaxes(x.reshape(2, 2, pw // 8, 8, 256), 1, 2).reshape(2, 2 * pw, 256)
            for part in range(2):
                first = pl.multiple_of((f * 2 + part) * 256 + i * 2 * pw, 2 * pw)
                vv[pl.ds(first, 2 * pw), :] = x[part].astype(BF16)
        return c

    lax.fori_loop(0, n_j, order, 0)
    loads[1].wait()

    def adjoint(f):
        base = pl.multiple_of(f * 512, 512)
        vr = vv[pl.ds(base, 256), :]
        vi = vv[pl.ds(base + 256, 256), :]
        kr = kv[pl.ds(base, 256), :]
        ki = kv[pl.ds(base + 256, 256), :]
        return nn(vr, kr) + nn(vi, ki), nn(vi, kr) - nn(vr, ki)

    def put(ref, parts):
        for c in range(2):
            for q in range(2):
                for h in range(2):
                    ref[q, h, c * 128:(c + 1) * 128, :] = parts[c][
                        q * 128:(q + 1) * 128, h * 128:(h + 1) * 128
                    ].astype(ref.dtype)

    put(s0, adjoint(other))
    met = n_xy - 1 + 4 + jnp.where(inland, 1, 0)
    pl.semaphore_wait(barrier, met + 2 * zh)
    signal(zpart)
    signal(zpair)

    def core_rs(q):
        return remote(s0.at[q], r0.at[q], core_s.at[q], core_r.at[q], sib)

    for q in batches:
        core_rs(q).start()
    loads[2].wait()
    loads[3].wait()
    dsend[0] = jnp.broadcast_to(d_ref[:, 128:256], (8, 128))
    dsend[1] = jnp.broadcast_to(d_ref[:, 0:128], (8, 128))
    up_dev = (jnp.minimum(row + 1, n_row - 1), col)
    down_dev = (jnp.maximum(row - 1, 0), col)
    up = [
        remote(kv.at[:, pl.ds(128, 128)], kh.at[:, pl.ds(0, 128)], halo_s.at[0], halo_r.at[0], up_dev),
        remote(dsend.at[0], dh.at[0], halo_s.at[1], halo_r.at[1], up_dev),
    ]
    down = [
        remote(kv.at[:, pl.ds(0, 128)], kh.at[:, pl.ds(128, 128)], halo_s.at[2], halo_r.at[2], down_dev),
        remote(dsend.at[1], dh.at[1], halo_s.at[3], halo_r.at[3], down_dev),
    ]

    @pl.when(row < n_row - 1)
    def _():
        for cp in up:
            cp.start()

    @pl.when(row > 0)
    def _():
        for cp in down:
            cp.start()

    put(ao, adjoint(core))

    def rows_of(t):
        return pl.ds(pl.multiple_of(lax.div(t, 2) * n_cb, n_cb), n_cb)

    slot = pl.ds(pl.multiple_of(cxy * n_cb, n_cb), n_cb)
    span = pl.ds(0, (n_xy - 1) * n_cb)
    lanes = lax.rem(cxy, 2)

    for q in batches:
        core_rs(q).wait_recv()
        s1[q] = (ao[q] + r0[q].astype(F32)).astype(BF16)

        def rs_start(i, c):
            t, dev = xy_dev(i)
            remote(
                s1.at[q, lax.rem(t, 2), rows_of(t)], r1.at[q, slot], rs_s.at[q], rs_r.at[q], dev
            ).start()
            return c

        lax.fori_loop(0, n_xy - 1, rs_start, 0)
        r1[q, slot, :] = s1[q, lanes, rows_of(cxy), :]

    @pl.when(row > 0)
    def _():
        for cp in up:
            cp.wait_recv()

    @pl.when(row < n_row - 1)
    def _():
        for cp in down:
            cp.wait_recv()

    @pl.when(row == 0)
    def _():
        kh[:, 0:128] = jnp.zeros((1024, 128), BF16)
        dh[0] = jnp.zeros((8, 128), F32)

    @pl.when(row == n_row - 1)
    def _():
        kh[:, 128:256] = jnp.zeros((1024, 128), BF16)
        dh[1] = jnp.zeros((8, 128), F32)

    lane = lax.broadcasted_iota(jnp.int32, (256, 256), 1)
    depth = lax.broadcasted_iota(jnp.int32, (256, 256), 0)
    d = d_ref[...]
    before = jnp.concatenate([dh[0, 0:1, :], d, dh[1, 0:1, :]], axis=1)
    left = pltpu.roll(before, 1, 1)[:, 128:384]
    right = pltpu.roll(before, 511, 1)[:, 128:384]
    ends = (lane == 0) & (row == 0) | (lane == 255) & (row == n_row - 1)

    def banded(gap):
        m = jnp.where(gap == 0, d * d + jnp.where(ends, 1.0, 2.0), 0.0)
        m = jnp.where(gap == -1, -(left + d), m)
        m = jnp.where(gap == 1, -(right + d), m)
        return jnp.where((gap == 2) | (gap == -2), 1.0, m)

    def thirds(m):
        a = m.astype(BF16)
        rest = m - a.astype(F32)
        b = rest.astype(BF16)
        return a, b, (rest - b.astype(F32)).astype(BF16)

    inner = thirds(banded(depth - lane))
    outer = thirds(banded(jnp.where(depth < 128, depth - 128, depth + 128) - lane))
    for i in range(0, 1024, 256):
        e = kv[i:i + 256, :]
        h = kh[i:i + 256, :]
        total = nn(e, inner[0]) + nn(h, outer[0])
        total = total + (nn(e, inner[1]) + nn(h, outer[1]))
        total = total + (nn(e, inner[2]) + nn(h, outer[2]))
        kp[b, i:i + 256, :] = total.astype(BF16)

    def swap(f):
        part = kp.at[b, pl.ds(pl.multiple_of(f * 512, 512), 512)]
        return remote(part, part, kx_s.at[f], kx_r.at[f], pair)


    def z_copies(q):
        return [
            remote(zs.at[q], zr.at[q, i], z_s.at[q], z_r.at[q], dev)
            for i, dev in enumerate((zpart, zpair, pair))
        ]

    def z_all(q):
        return remote(zr.at[q], zr.at[q], z_s.at[q], z_r.at[q], sib)

    @pl.when(zh == 0)
    def _():
        pl.semaphore_wait(barrier, 2)

    own = []
    for q in batches:
        remote(r1.at[q, span], r1.at[q, span], rs_s.at[q], rs_r.at[q], sib).wait_recv()
        acc = r1[q, 0:n_cb, :].astype(F32)
        for s in range(1, n_xy):
            acc = acc + r1[q, s * n_cb:(s + 1) * n_cb, :].astype(F32)
        zs[q] = acc.astype(BF16)
        for cp in z_copies(q):
            cp.start()
        own.append(acc)

    swap(core).start()

    @pl.when(zh == 0)
    def _():
        swap(other).start()

    for q, acc in zip(batches, own):
        z_all(q).wait_recv()

        def share(x):
            return jnp.where(b == 0, x[0:8, :], x[8:16, :])

        mine = share(acc + zr[q, 0].astype(F32))
        theirs = share(zr[q, 1].astype(F32) + zr[q, 2].astype(F32))
        even = jnp.where(b == 0, mine, theirs)
        odd = jnp.where(b == 0, theirs, mine)
        final = jnp.concatenate([even, odd], axis=0).astype(BF16)
        fc[q] = final

        def ag_start(i, c):
            _, dev = xy_dev(i)
            remote(
                fc.at[q], g.at[core, q, lanes, rows_of(cxy)], ag_s.at[q], ag_r.at[q], dev
            ).start()
            return c

        lax.fori_loop(0, n_xy - 1, ag_start, 0)
        g[core, q, lanes, rows_of(cxy), :] = final

    @pl.when(zh == 1)
    def _():
        swap(other).start()

    def cag(f, q):
        return remote(g.at[f, q], g.at[f, q], cag_s.at[q], cag_r.at[q], sib)

    def forward(f, q):
        base = pl.multiple_of(f * 512, 512)
        both = jnp.concatenate([g[f, q, 0], g[f, q, 1]], axis=1).astype(F32).reshape(16, 2, 8, 256)
        real = imag = 0.0
        for block in range(2):
            x = both[:, block].reshape(128, 256).astype(BF16)
            real = real + nt(x, kp[block, pl.ds(base, 256), :])
            imag = imag + nt(x, kp[block, pl.ds(base + 256, 256), :])
        hr = (real[0:64, :] - imag[64:128, :]).astype(BF16)
        hi = (imag[0:64, :] + real[64:128, :]).astype(BF16)
        for aa in range(2):
            hs[q, f, aa, 0:pw, :] = hr[aa * pw:(aa + 1) * pw, :]
            hs[q, f, aa, pw:2 * pw, :] = hi[aa * pw:(aa + 1) * pw, :]

        @pl.when(q == half)
        def _():
            near(f).start()

        @pl.when((q != half) & (a == 1))
        def _():
            give(f).start()

    def near(f):
        return remote(hs.at[half, f, 1 - a], r2.at[f], h_s.at[f], h_r.at[f], mate)

    def give(f):
        return remote(hs.at[1 - half, f, 1 - a], rg.at[f], g_s.at[f], g_r.at[f], mate)

    def across(f):
        return remote(l2s.at[f], rc.at[f], cr_s.at[f], cr_r.at[f], beyond)

    def cross(giving):
        for f in (core, other):
            give(f).wait_recv()
            l2s[f] = (hs[1 - half, f, a].astype(F32) + rg[f].astype(F32)).astype(BF16)
            across(f).start()
            if giving:
                give(f).start()

    for q in batches:
        remote(r1.at[q, span], r1.at[q, span], ag_s.at[q], ag_r.at[q], sib).wait_recv()
        cag(core, q).start()
        if q == 0:
            swap(core).wait_recv()
        forward(core, q)
        cag(other, q).wait_recv()
        if q == 0:
            swap(other).wait_recv()
        forward(other, q)

        @pl.when((q != half) & (a == 0))
        def _():
            cross(True)

    @pl.when(a == 1)
    def _():
        cross(False)

    for f in (core, other):
        near(f).wait_recv()
        total = hs[half, f, a].astype(F32) + r2[f].astype(F32)
        across(f).wait_recv()
        total = total + rc[f].astype(F32)
        level = nv_ref[pl.ds(f, 1), :]
        for c in range(2):
            first = pl.multiple_of(f * 512 + c * 256 + half * 128 + a * 64, 64)
            block = vv[pl.ds(first, 2 * pw), :].astype(F32).reshape(pw // 8, 2, 8, 256)
            mine = jnp.where(b == 0, block[:, 0], block[:, 1]).reshape(pw, 256)
            o_ref[pl.ds(pl.multiple_of((f * 2 + c) * pw, pw), pw), :] = (
                total[c * pw:(c + 1) * pw, :] + level * mine
            )

    @pl.when(row < n_row - 1)
    def _():
        for cp in up:
            cp.wait_send()

    @pl.when(row > 0)
    def _():
        for cp in down:
            cp.wait_send()

    for q in range(2):
        core_rs(q).wait_send()
        remote(r1.at[q, span], r1.at[q, span], rs_s.at[q], rs_r.at[q], sib).wait_send()
        z_all(q).wait_send()
        remote(r1.at[q, span], r1.at[q, span], ag_s.at[q], ag_r.at[q], sib).wait_send()
        cag(core, q).wait_send()
        swap(q).wait_send()
        near(q).wait_send()
        give(q).wait_send()
        across(q).wait_send()


def shards(kernel, probes, noise_var, prior_diag):
    n_row = lax.axis_size("row")
    n_col = lax.axis_size("col")
    n_j = n_row // 2
    pw = 256 // n_row
    n_cb = 512 // (n_col // 4)
    k = kernel.reshape(1024, 256)
    vmem = pl.BlockSpec(memory_space=pltpu.VMEM)
    hbm = pl.BlockSpec(memory_space=pltpu.HBM)
    dma = pltpu.SemaphoreType.DMA
    out = pl.pallas_call(
        functools.partial(body, n_row, n_col),
        out_shape=jax.ShapeDtypeStruct((4 * pw, 256), F32),
        in_specs=[hbm, hbm, hbm, hbm],
        out_specs=vmem,
        scratch_shapes=[
            pltpu.VMEM((1024, 256), BF16),
            pltpu.VMEM((256, 2, 2, 256), BF16),
            pltpu.VMEM((1024, 256), BF16),
            pltpu.VMEM((2, 256), F32),
            pltpu.VMEM((1, 256), F32),
            pltpu.VMEM((1024, 256), BF16),
            pltpu.VMEM((2, 8, 128), F32),
            pltpu.VMEM((2, 8, 128), F32),
            pltpu.VMEM((2, 1024, 256), BF16),
            pltpu.VMEM((2, 2, 256, 128), BF16),
            pltpu.VMEM((2, 2, 256, 128), BF16),
            pltpu.VMEM((2, 2, 256, 128), F32),
            pltpu.VMEM((2, 2, 256, 128), BF16),
            pltpu.VMEM((2, 512, 128), BF16),
            pltpu.VMEM((2, n_cb, 128), BF16),
            pltpu.VMEM((2, 3, n_cb, 128), BF16),
            pltpu.VMEM((2, n_cb, 128), BF16),
            pltpu.VMEM((2, 2, 2, 256, 128), BF16),
            pltpu.VMEM((2, 2, n_j // 2, 2 * pw, 256), BF16),
            pltpu.VMEM((2, 2 * pw, 256), BF16),
            pltpu.VMEM((2, 2 * pw, 256), BF16),
            pltpu.VMEM((2, 2 * pw, 256), BF16),
            pltpu.VMEM((2, 2 * pw, 256), BF16),
            dma((4,)), dma((4,)), dma((4,)), dma((2,)), dma((2,)), dma((2,)), dma((2,)), dma((2,)),
            dma((2,)), dma((2,)), dma((2,)), dma((2,)), dma((2,)),
            dma((2,)), dma((2,)), dma((2,)), dma((2,)), dma((2,)), dma((2,)), dma((2,)), dma((2,)),
        ],
        compiler_params=pltpu.CompilerParams(
            collective_id=0, has_side_effects=True, vmem_limit_bytes=60 * 1024 * 1024
        ),
    )(k, probes, noise_var, prior_diag.reshape(1, 256))
    return jnp.transpose(out.reshape(2, 2, pw, 256), (2, 0, 1, 3))


def solution(mesh):
    in_specs = (P(None, None, "col", "row"), P(None, None, None, "col"), P(None, "col"), P("row"))
    out_specs = P("row", None, None, "col")
    return jax.shard_map(shards, mesh=mesh, in_specs=in_specs, out_specs=out_specs, check_vma=False)
```

```python
import functools

import jax
import jax.numpy as jnp
from jax import lax
from jax.experimental import pallas as pl
from jax.experimental.pallas import tpu as pltpu
from jax.sharding import PartitionSpec as P

F32 = jnp.float32
BF16 = jnp.bfloat16
MESH = pl.DeviceIdType.MESH


def nt(a, b):
    return lax.dot_general(a, b, (((1,), (1,)), ((), ())), preferred_element_type=F32)


def nn(a, b):
    return jnp.dot(a, b, preferred_element_type=F32)


def body(
    n_row, n_col,
    k_hbm, v_hbm, nv_hbm, d_hbm, o_ref,
    kv, vraw, vv, nv_ref, d_ref, kh, dsend, dh, ks, kp, s0, r0, ao, s1, r1, zs, zr, fc, g, hs, r2, rg, l2s, rc, rd, xs, rl,
    load_sem, halo_s, halo_r, core_s, core_r, rs_s, rs_r, z_s, z_r, ag_s, ag_r, kc_s, kc_r,
    kx_s, kx_r, h_s, h_r, g_s, g_r, cr_s, cr_r, fa_s, fa_r, lo_s, lo_r,
):
    row = lax.axis_index("row")
    col = lax.axis_index("col")
    n_xy = n_col // 4
    n_j = n_row // 2
    core = lax.rem(col, 2)
    zh = lax.rem(lax.div(col, 2), 2)
    cxy = lax.div(col, 4)
    half = lax.div(row, n_j)
    j = lax.rem(row, n_j)
    a = lax.div(j, 2)
    b = lax.rem(j, 2)
    n_cb = 512 // n_xy
    pw = 256 // n_row
    other = 1 - core
    batches = (0, 1)
    order_of_rows = (1, 0)

    sib = (row, cxy * 4 + zh * 2 + other)
    pair_row = row + 1 - 2 * b
    pair = (pair_row, col)
    zcol = cxy * 4 + (1 - zh) * 2 + core
    zpart = (row, zcol)
    zpair = (pair_row, zcol)
    mate = (half * n_j + (1 - a) * 2 + b, col)
    beyond = ((1 - half) * n_j + j, col)
    aslant = ((1 - half) * n_j + (1 - a) * 2 + b, col)

    def col_of(r):
        return cxy * 4 + zh * 2 + r

    def xy_dev(i):
        step = lax.div(i + 1, 2)
        k = n_xy // 2 + jnp.where(lax.rem(i, 2) == 1, -step, step)
        t = lax.rem(cxy + k, n_xy)
        return t, (row, t * 4 + zh * 2 + core)

    def remote(src, dst, ss, rs, dev):
        return pltpu.make_async_remote_copy(
            src_ref=src, dst_ref=dst, send_sem=ss, recv_sem=rs, device_id=dev, device_id_type=MESH
        )

    barrier = pltpu.get_barrier_semaphore()

    def signal(dev):
        pl.semaphore_signal(barrier, inc=1, device_id=dev, device_id_type=MESH)

    def sig_xy(i, c):
        signal(xy_dev(i)[1])
        return c

    lax.fori_loop(0, n_xy - 1, sig_xy, 0)
    signal(beyond)
    signal(aslant)
    signal((aslant[0], col_of(other)))
    signal(mate)
    signal((beyond[0], col_of(other)))
    signal((mate[0], col_of(other)))
    signal(pair)
    signal(sib)
    inland = (row > 0) & (row < n_row - 1)

    @pl.when(inland)
    def _():
        signal((row - 1 + 2 * b, col))

    loads = [
        pltpu.make_async_copy(src, dst, load_sem.at[i])
        for i, (src, dst) in enumerate(
            ((v_hbm, vraw), (k_hbm, kv), (d_hbm, d_ref), (nv_hbm, nv_ref))
        )
    ]
    for cp in loads:
        cp.start()

    loads[0].wait()

    def order(i, c):
        for f in range(2):
            x = jnp.swapaxes(vraw[pl.ds(i * 2 * pw, 2 * pw), f].astype(F32), 0, 1)
            x = jnp.swapaxes(x.reshape(2, 2, pw // 8, 8, 256), 1, 2).reshape(2, 2 * pw, 256)
            for part in range(2):
                first = pl.multiple_of((f * 2 + part) * 256 + i * 2 * pw, 2 * pw)
                vv[pl.ds(first, 2 * pw), :] = x[part].astype(BF16)
        return c

    lax.fori_loop(0, n_j, order, 0)
    loads[1].wait()

    def adjoint(f):
        base = pl.multiple_of(f * 512, 512)
        vr = vv[pl.ds(base, 256), :]
        vi = vv[pl.ds(base + 256, 256), :]
        kr = kv[pl.ds(base, 256), :]
        ki = kv[pl.ds(base + 256, 256), :]
        return nn(vr, kr) + nn(vi, ki), nn(vi, kr) - nn(vr, ki)

    def put(ref, parts):
        for c in range(2):
            for q in range(2):
                for h in range(2):
                    ref[q, h, c * 128:(c + 1) * 128, :] = parts[c][
                        q * 128:(q + 1) * 128, h * 128:(h + 1) * 128
                    ].astype(ref.dtype)

    put(s0, adjoint(other))
    met = n_xy - 1 + 8 + jnp.where(inland, 1, 0)
    pl.semaphore_wait(barrier, met + 2 * zh)
    signal(zpart)
    signal(zpair)

    def core_rs(q):
        return remote(s0.at[q], r0.at[q], core_s.at[q], core_r.at[q], sib)

    for q in batches:
        core_rs(q).start()
    loads[2].wait()
    loads[3].wait()
    dsend[0] = jnp.broadcast_to(d_ref[:, 128:256], (8, 128))
    dsend[1] = jnp.broadcast_to(d_ref[:, 0:128], (8, 128))
    up_dev = (jnp.minimum(row + 1, n_row - 1), col)
    down_dev = (jnp.maximum(row - 1, 0), col)
    up = [
        remote(kv.at[:, pl.ds(128, 128)], kh.at[:, pl.ds(0, 128)], halo_s.at[0], halo_r.at[0], up_dev),
        remote(dsend.at[0], dh.at[0], halo_s.at[1], halo_r.at[1], up_dev),
    ]
    down = [
        remote(kv.at[:, pl.ds(0, 128)], kh.at[:, pl.ds(128, 128)], halo_s.at[2], halo_r.at[2], down_dev),
        remote(dsend.at[1], dh.at[1], halo_s.at[3], halo_r.at[3], down_dev),
    ]

    @pl.when(row < n_row - 1)
    def _():
        for cp in up:
            cp.start()

    @pl.when(row > 0)
    def _():
        for cp in down:
            cp.start()

    put(ao, adjoint(core))

    def rows_of(t):
        return pl.ds(pl.multiple_of(lax.div(t, 2) * n_cb, n_cb), n_cb)

    slot = pl.ds(pl.multiple_of(cxy * n_cb, n_cb), n_cb)
    span = pl.ds(0, (n_xy - 1) * n_cb)
    lanes = lax.rem(cxy, 2)

    for q in batches:
        core_rs(q).wait_recv()
        s1[q] = (ao[q] + r0[q].astype(F32)).astype(BF16)

        def rs_start(i, c):
            t, dev = xy_dev(i)
            remote(
                s1.at[q, lax.rem(t, 2), rows_of(t)], r1.at[q, slot], rs_s.at[q], rs_r.at[q], dev
            ).start()
            return c

        lax.fori_loop(0, n_xy - 1, rs_start, 0)
        r1[q, slot, :] = s1[q, lanes, rows_of(cxy), :]

    @pl.when(row > 0)
    def _():
        for cp in up:
            cp.wait_recv()

    @pl.when(row < n_row - 1)
    def _():
        for cp in down:
            cp.wait_recv()

    @pl.when(row == 0)
    def _():
        kh[:, 0:128] = jnp.zeros((1024, 128), BF16)
        dh[0] = jnp.zeros((8, 128), F32)

    @pl.when(row == n_row - 1)
    def _():
        kh[:, 128:256] = jnp.zeros((1024, 128), BF16)
        dh[1] = jnp.zeros((8, 128), F32)

    lane = lax.broadcasted_iota(jnp.int32, (256, 256), 1)
    depth = lax.broadcasted_iota(jnp.int32, (256, 256), 0)
    d = d_ref[...]
    before = jnp.concatenate([dh[0, 0:1, :], d, dh[1, 0:1, :]], axis=1)
    left = pltpu.roll(before, 1, 1)[:, 128:384]
    right = pltpu.roll(before, 511, 1)[:, 128:384]
    ends = (lane == 0) & (row == 0) | (lane == 255) & (row == n_row - 1)

    def banded(gap):
        m = jnp.where(gap == 0, d * d + jnp.where(ends, 1.0, 2.0), 0.0)
        m = jnp.where(gap == -1, -(left + d), m)
        m = jnp.where(gap == 1, -(right + d), m)
        return jnp.where((gap == 2) | (gap == -2), 1.0, m)

    def thirds(m):
        a = m.astype(BF16)
        rest = m - a.astype(F32)
        b = rest.astype(BF16)
        return a, b, (rest - b.astype(F32)).astype(BF16)

    inner = thirds(banded(depth - lane))
    outer = thirds(banded(jnp.where(depth < 128, depth - 128, depth + 128) - lane))

    def smooth(f, part):
        rows = pl.ds(pl.multiple_of(f * 512 + part * 256, 256), 256)
        e = kv[rows, :]
        h = kh[rows, :]
        total = nn(e, inner[0]) + nn(h, outer[0])
        total = total + (nn(e, inner[1]) + nn(h, outer[1]))
        total = total + (nn(e, inner[2]) + nn(h, outer[2]))
        return total.astype(BF16)

    core_swap = remote(ks, kp.at[b, core], kc_s, kc_r, sib)
    for part in range(2):
        ks[part * 256:(part + 1) * 256, :] = smooth(other, part)
    core_swap.start()
    for part in range(2):
        kp[b, core, part * 256:(part + 1) * 256, :] = smooth(core, part)

    def swap(r):
        return remote(kp.at[b, r], kp.at[b, r], kx_s.at[r], kx_r.at[r], pair)

    def z_copies(q):
        return [
            remote(zs.at[q], zr.at[q, i], z_s.at[q], z_r.at[q], dev)
            for i, dev in enumerate((zpart, zpair, pair))
        ]

    def z_all(q):
        return remote(zr.at[q], zr.at[q], z_s.at[q], z_r.at[q], sib)

    @pl.when(zh == 0)
    def _():
        pl.semaphore_wait(barrier, 2)

    own = []
    for q in batches:
        remote(r1.at[q, span], r1.at[q, span], rs_s.at[q], rs_r.at[q], sib).wait_recv()
        acc = r1[q, 0:n_cb, :].astype(F32)
        for s in range(1, n_xy):
            acc = acc + r1[q, s * n_cb:(s + 1) * n_cb, :].astype(F32)
        zs[q] = acc.astype(BF16)
        for cp in z_copies(q):
            cp.start()
        own.append(acc)

    swap(core).start()
    core_swap.wait_recv()

    @pl.when(zh == 0)
    def _():
        swap(other).start()

    for q, acc in zip(batches, own):
        z_all(q).wait_recv()

        def share(x):
            return jnp.where(b == 0, x[0:8, :], x[8:16, :])

        mine = share(acc + zr[q, 0].astype(F32))
        theirs = share(zr[q, 1].astype(F32) + zr[q, 2].astype(F32))
        even = jnp.where(b == 0, mine, theirs)
        odd = jnp.where(b == 0, theirs, mine)
        final = jnp.concatenate([even, odd], axis=0).astype(BF16)
        fc[q] = final

        def ag_start(i, c):
            _, dev = xy_dev(i)
            remote(
                fc.at[q], g.at[q, lanes, rows_of(cxy)], ag_s.at[q], ag_r.at[q], dev
            ).start()
            return c

        lax.fori_loop(0, n_xy - 1, ag_start, 0)
        g[q, lanes, rows_of(cxy), :] = final

    @pl.when(zh == 1)
    def _():
        swap(other).start()

    def forward(r, q):
        both = jnp.concatenate([g[q, 0], g[q, 1]], axis=1).astype(F32).reshape(16, 2, 8, 256)
        real = imag = 0.0
        for block in range(2):
            x = both[:, block].reshape(128, 256).astype(BF16)
            real = real + nt(x, kp[block, r, 0:256, :])
            imag = imag + nt(x, kp[block, r, 256:512, :])
        hr = (real[0:64, :] - imag[64:128, :]).astype(BF16)
        hi = (imag[0:64, :] + real[64:128, :]).astype(BF16)
        for aa in range(2):
            hs[q, r, aa, 0:pw, :] = hr[aa * pw:(aa + 1) * pw, :]
            hs[q, r, aa, pw:2 * pw, :] = hi[aa * pw:(aa + 1) * pw, :]

        @pl.when(q == half)
        def _():
            near(r).start()

        @pl.when((q != half) & (a == 1))
        def _():
            give(r).start()

        @pl.when(q != half)
        def _():
            far(r).start()

    def near(r):
        return remote(
            hs.at[half, r, 1 - a], r2.at[core], h_s.at[r], h_r.at[core], (mate[0], col_of(r))
        )

    def far(r):
        return remote(
            hs.at[1 - half, r, 1], rd.at[core, a], fa_s.at[r], fa_r.at[core],
            ((1 - half) * n_j + 2 + b, col_of(r)),
        )

    def give(r):
        return remote(hs.at[1 - half, r, 0], rg.at[r], g_s.at[r], g_r.at[r], mate)

    def across(r):
        return remote(l2s.at[r], rc.at[core], cr_s.at[r], cr_r.at[core], (beyond[0], col_of(r)))

    def local():
        return remote(hs.at[half, other, a], rl, lo_s, lo_r, sib)

    def cross():
        for r in order_of_rows:
            give(r).wait_recv()
            l2s[r] = (hs[1 - half, r, 0].astype(F32) + rg[r].astype(F32)).astype(BF16)
            across(r).start()

    for q in batches:
        remote(r1.at[q, span], r1.at[q, span], ag_s.at[q], ag_r.at[q], sib).wait_recv()
        if q == 0:
            swap(core).wait_recv()
            swap(other).wait_recv()
        for r in order_of_rows:
            forward(r, q)

        @pl.when(q == half)
        def _():
            local().start()

        @pl.when((q != half) & (a == 0))
        def _():
            cross()

    for f in (core, other):
        if f is core:
            total = hs[half, core, a].astype(F32)
        else:
            local().wait_recv()
            total = rl[...].astype(F32)
        remote(r2.at[f], r2.at[f], h_s.at[f], h_r.at[f], sib).wait_recv()
        total = total + r2[f].astype(F32)

        @pl.when(a == 0)
        def _():
            remote(rc.at[f], rc.at[f], cr_s.at[f], cr_r.at[f], sib).wait_recv()
            xs[...] = rc[f].astype(F32)

        @pl.when(a == 1)
        def _():
            remote(rd.at[f], rd.at[f], fa_s.at[f], fa_r.at[f], sib).wait_recv()
            xs[...] = rd[f, 0].astype(F32) + rd[f, 1].astype(F32)

        total = total + xs[...]
        level = nv_ref[pl.ds(f, 1), :]
        for c in range(2):
            first = pl.multiple_of(f * 512 + c * 256 + half * 128 + a * 64, 64)
            block = vv[pl.ds(first, 2 * pw), :].astype(F32).reshape(pw // 8, 2, 8, 256)
            mine = jnp.where(b == 0, block[:, 0], block[:, 1]).reshape(pw, 256)
            o_ref[pl.ds(pl.multiple_of((f * 2 + c) * pw, pw), pw), :] = (
                total[c * pw:(c + 1) * pw, :] + level * mine
            )

    @pl.when(row < n_row - 1)
    def _():
        for cp in up:
            cp.wait_send()

    @pl.when(row > 0)
    def _():
        for cp in down:
            cp.wait_send()

    for q in range(2):
        core_rs(q).wait_send()
        remote(r1.at[q, span], r1.at[q, span], rs_s.at[q], rs_r.at[q], sib).wait_send()
        z_all(q).wait_send()
        remote(r1.at[q, span], r1.at[q, span], ag_s.at[q], ag_r.at[q], sib).wait_send()
        swap(q).wait_send()
        near(q).wait_send()
        far(q).wait_send()

        @pl.when(a == 1)
        def _():
            give(q).wait_send()

        @pl.when(a == 0)
        def _():
            across(q).wait_send()

    core_swap.wait_send()
    local().wait_send()


def shards(kernel, probes, noise_var, prior_diag):
    n_row = lax.axis_size("row")
    n_col = lax.axis_size("col")
    n_j = n_row // 2
    pw = 256 // n_row
    n_cb = 512 // (n_col // 4)
    k = kernel.reshape(1024, 256)
    vmem = pl.BlockSpec(memory_space=pltpu.VMEM)
    hbm = pl.BlockSpec(memory_space=pltpu.HBM)
    dma = pltpu.SemaphoreType.DMA
    out = pl.pallas_call(
        functools.partial(body, n_row, n_col),
        out_shape=jax.ShapeDtypeStruct((4 * pw, 256), F32),
        in_specs=[hbm, hbm, hbm, hbm],
        out_specs=vmem,
        scratch_shapes=[
            pltpu.VMEM((1024, 256), BF16),
            pltpu.VMEM((256, 2, 2, 256), BF16),
            pltpu.VMEM((1024, 256), BF16),
            pltpu.VMEM((2, 256), F32),
            pltpu.VMEM((1, 256), F32),
            pltpu.VMEM((1024, 256), BF16),
            pltpu.VMEM((2, 8, 128), F32),
            pltpu.VMEM((2, 8, 128), F32),
            pltpu.VMEM((512, 256), BF16),
            pltpu.VMEM((2, 2, 512, 256), BF16),
            pltpu.VMEM((2, 2, 256, 128), BF16),
            pltpu.VMEM((2, 2, 256, 128), BF16),
            pltpu.VMEM((2, 2, 256, 128), F32),
            pltpu.VMEM((2, 2, 256, 128), BF16),
            pltpu.VMEM((2, 512, 128), BF16),
            pltpu.VMEM((2, n_cb, 128), BF16),
            pltpu.VMEM((2, 3, n_cb, 128), BF16),
            pltpu.VMEM((2, n_cb, 128), BF16),
            pltpu.VMEM((2, 2, 256, 128), BF16),
            pltpu.VMEM((2, 2, n_j // 2, 2 * pw, 256), BF16),
            pltpu.VMEM((2, 2 * pw, 256), BF16),
            pltpu.VMEM((2, 2 * pw, 256), BF16),
            pltpu.VMEM((2, 2 * pw, 256), BF16),
            pltpu.VMEM((2, 2 * pw, 256), BF16),
            pltpu.VMEM((2, 2, 2 * pw, 256), BF16),
            pltpu.VMEM((2 * pw, 256), F32),
            pltpu.VMEM((2 * pw, 256), BF16),
            dma((4,)), dma((4,)), dma((4,)), dma((2,)), dma((2,)), dma((2,)), dma((2,)), dma((2,)),
            dma((2,)), dma((2,)), dma((2,)), dma, dma,
            dma((2,)), dma((2,)), dma((2,)), dma((2,)), dma((2,)), dma((2,)), dma((2,)), dma((2,)),
            dma((2,)), dma((2,)), dma, dma,
        ],
        compiler_params=pltpu.CompilerParams(
            collective_id=0, has_side_effects=True, vmem_limit_bytes=60 * 1024 * 1024
        ),
    )(k, probes, noise_var, prior_diag.reshape(1, 256))
    return jnp.transpose(out.reshape(2, 2, pw, 256), (2, 0, 1, 3))


def solution(mesh):
    in_specs = (P(None, None, "col", "row"), P(None, None, None, "col"), P(None, "col"), P("row"))
    out_specs = P("row", None, None, "col")
    return jax.shard_map(shards, mesh=mesh, in_specs=in_specs, out_specs=out_specs, check_vma=False)
```

```python
import functools

import jax
import jax.numpy as jnp
from jax import lax
from jax.experimental import pallas as pl
from jax.experimental.pallas import tpu as pltpu
from jax.sharding import PartitionSpec as P

F32 = jnp.float32
BF16 = jnp.bfloat16
MESH = pl.DeviceIdType.MESH


def nt(a, b):
    return lax.dot_general(a, b, (((1,), (1,)), ((), ())), preferred_element_type=F32)


def nn(a, b):
    return jnp.dot(a, b, preferred_element_type=F32)


def body(
    n_row, n_col,
    k_hbm, v_hbm, nv_hbm, d_hbm, o_ref,
    kv, vraw, vv, nv_ref, d_ref, kh, dsend, dh, ks, kp, s0, r0, ao, s1, r1, zs, zr, fc, g, hs, r2, rg, l2s, rc, rd, xs, rl,
    load_sem, halo_s, halo_r, core_s, core_r, rs_s, rs_r, z_s, z_r, ag_s, ag_r, kc_s, kc_r,
    kx_s, kx_r, h_s, h_r, g_s, g_r, cr_s, cr_r, fa_s, fa_r, lo_s, lo_r,
):
    row = lax.axis_index("row")
    col = lax.axis_index("col")
    n_xy = n_col // 4
    n_j = n_row // 2
    core = lax.rem(col, 2)
    zh = lax.rem(lax.div(col, 2), 2)
    cxy = lax.div(col, 4)
    half = lax.div(row, n_j)
    j = lax.rem(row, n_j)
    a = lax.div(j, 2)
    b = lax.rem(j, 2)
    n_cb = 512 // n_xy
    pw = 256 // n_row
    other = 1 - core
    batches = (0, 1)
    order_of_rows = (1, 0)

    sib = (row, cxy * 4 + zh * 2 + other)
    pair_row = row + 1 - 2 * b
    pair = (pair_row, col)
    zcol = cxy * 4 + (1 - zh) * 2 + core
    zpart = (row, zcol)
    zpair = (pair_row, zcol)
    mate = (half * n_j + (1 - a) * 2 + b, col)
    beyond = ((1 - half) * n_j + j, col)
    aslant = ((1 - half) * n_j + (1 - a) * 2 + b, col)

    def col_of(r):
        return cxy * 4 + zh * 2 + r

    def xy_dev(i):
        step = lax.div(i + 1, 2)
        k = n_xy // 2 + jnp.where(lax.rem(i, 2) == 1, -step, step)
        t = lax.rem(cxy + k, n_xy)
        return t, (row, t * 4 + zh * 2 + core)

    def remote(src, dst, ss, rs, dev):
        return pltpu.make_async_remote_copy(
            src_ref=src, dst_ref=dst, send_sem=ss, recv_sem=rs, device_id=dev, device_id_type=MESH
        )

    barrier = pltpu.get_barrier_semaphore()

    def signal(dev):
        pl.semaphore_signal(barrier, inc=1, device_id=dev, device_id_type=MESH)

    def sig_xy(i, c):
        signal(xy_dev(i)[1])
        return c

    lax.fori_loop(0, n_xy - 1, sig_xy, 0)
    signal(beyond)
    signal(aslant)
    signal((aslant[0], col_of(other)))
    signal(mate)
    signal((beyond[0], col_of(other)))
    signal((mate[0], col_of(other)))
    signal(pair)
    signal(sib)
    inland = (row > 0) & (row < n_row - 1)

    @pl.when(inland)
    def _():
        signal((row - 1 + 2 * b, col))

    loads = [
        pltpu.make_async_copy(src, dst, load_sem.at[i])
        for i, (src, dst) in enumerate(
            ((v_hbm, vraw), (k_hbm, kv), (d_hbm, d_ref), (nv_hbm, nv_ref))
        )
    ]
    for cp in loads:
        cp.start()

    loads[0].wait()

    def order(i, c):
        for f in range(2):
            x = jnp.swapaxes(vraw[pl.ds(i * 2 * pw, 2 * pw), f].astype(F32), 0, 1)
            x = jnp.swapaxes(x.reshape(2, 2, pw // 8, 8, 256), 1, 2).reshape(2, 2 * pw, 256)
            for part in range(2):
                first = pl.multiple_of((f * 2 + part) * 256 + i * 2 * pw, 2 * pw)
                vv[pl.ds(first, 2 * pw), :] = x[part].astype(BF16)
        return c

    lax.fori_loop(0, n_j, order, 0)
    loads[1].wait()

    def adjoint(f):
        base = pl.multiple_of(f * 512, 512)
        vr = vv[pl.ds(base, 256), :]
        vi = vv[pl.ds(base + 256, 256), :]
        kr = kv[pl.ds(base, 256), :]
        ki = kv[pl.ds(base + 256, 256), :]
        return nn(vr, kr) + nn(vi, ki), nn(vi, kr) - nn(vr, ki)

    def put(ref, parts):
        for c in range(2):
            for q in range(2):
                for h in range(2):
                    ref[q, h, c * 128:(c + 1) * 128, :] = parts[c][
                        q * 128:(q + 1) * 128, h * 128:(h + 1) * 128
                    ].astype(ref.dtype)

    put(s0, adjoint(other))
    met = n_xy - 1 + 8 + jnp.where(inland, 1, 0)
    pl.semaphore_wait(barrier, met + 2 * zh)
    signal(zpart)
    signal(zpair)

    def core_rs(q):
        return remote(s0.at[q], r0.at[q], core_s.at[q], core_r.at[q], sib)

    for q in batches:
        core_rs(q).start()
    loads[2].wait()
    loads[3].wait()
    dsend[0] = jnp.broadcast_to(d_ref[:, 128:256], (8, 128))
    dsend[1] = jnp.broadcast_to(d_ref[:, 0:128], (8, 128))
    up_dev = (jnp.minimum(row + 1, n_row - 1), col)
    down_dev = (jnp.maximum(row - 1, 0), col)
    up = [
        remote(kv.at[:, pl.ds(128, 128)], kh.at[:, pl.ds(0, 128)], halo_s.at[0], halo_r.at[0], up_dev),
        remote(dsend.at[0], dh.at[0], halo_s.at[1], halo_r.at[1], up_dev),
    ]
    down = [
        remote(kv.at[:, pl.ds(0, 128)], kh.at[:, pl.ds(128, 128)], halo_s.at[2], halo_r.at[2], down_dev),
        remote(dsend.at[1], dh.at[1], halo_s.at[3], halo_r.at[3], down_dev),
    ]

    @pl.when(row < n_row - 1)
    def _():
        for cp in up:
            cp.start()

    @pl.when(row > 0)
    def _():
        for cp in down:
            cp.start()

    put(ao, adjoint(core))

    def rows_of(t):
        return pl.ds(pl.multiple_of(lax.div(t, 2) * n_cb, n_cb), n_cb)

    slot = pl.ds(pl.multiple_of(cxy * n_cb, n_cb), n_cb)
    span = pl.ds(0, (n_xy - 1) * n_cb)
    lanes = lax.rem(cxy, 2)

    for q in batches:
        core_rs(q).wait_recv()
        s1[q] = (ao[q] + r0[q].astype(F32)).astype(BF16)

        def rs_start(i, c):
            t, dev = xy_dev(i)
            remote(
                s1.at[q, lax.rem(t, 2), rows_of(t)], r1.at[q, slot], rs_s.at[q], rs_r.at[q], dev
            ).start()
            return c

        lax.fori_loop(0, n_xy - 1, rs_start, 0)
        r1[q, slot, :] = s1[q, lanes, rows_of(cxy), :]

    @pl.when(row > 0)
    def _():
        for cp in up:
            cp.wait_recv()

    @pl.when(row < n_row - 1)
    def _():
        for cp in down:
            cp.wait_recv()

    @pl.when(row == 0)
    def _():
        kh[:, 0:128] = jnp.zeros((1024, 128), BF16)
        dh[0] = jnp.zeros((8, 128), F32)

    @pl.when(row == n_row - 1)
    def _():
        kh[:, 128:256] = jnp.zeros((1024, 128), BF16)
        dh[1] = jnp.zeros((8, 128), F32)

    lane = lax.broadcasted_iota(jnp.int32, (256, 256), 1)
    depth = lax.broadcasted_iota(jnp.int32, (256, 256), 0)
    d = d_ref[...]
    before = jnp.concatenate([dh[0, 0:1, :], d, dh[1, 0:1, :]], axis=1)
    left = pltpu.roll(before, 1, 1)[:, 128:384]
    right = pltpu.roll(before, 511, 1)[:, 128:384]
    ends = (lane == 0) & (row == 0) | (lane == 255) & (row == n_row - 1)

    def banded(gap):
        m = jnp.where(gap == 0, d * d + jnp.where(ends, 1.0, 2.0), 0.0)
        m = jnp.where(gap == -1, -(left + d), m)
        m = jnp.where(gap == 1, -(right + d), m)
        return jnp.where((gap == 2) | (gap == -2), 1.0, m)

    def thirds(m):
        a = m.astype(BF16)
        rest = m - a.astype(F32)
        b = rest.astype(BF16)
        return a, b, (rest - b.astype(F32)).astype(BF16)

    inner = thirds(banded(depth - lane))
    outer = thirds(banded(jnp.where(depth < 128, depth - 128, depth + 128) - lane))

    def smooth(f, part):
        rows = pl.ds(pl.multiple_of(f * 512 + part * 256, 256), 256)
        e = kv[rows, :]
        h = kh[rows, :]
        total = nn(e, inner[0]) + nn(h, outer[0])
        total = total + (nn(e, inner[1]) + nn(h, outer[1]))
        total = total + (nn(e, inner[2]) + nn(h, outer[2]))
        return total.astype(BF16)

    core_swap = remote(ks, kp.at[b, core], kc_s, kc_r, sib)
    for part in range(2):
        ks[part * 256:(part + 1) * 256, :] = smooth(other, part)
    core_swap.start()
    for part in range(2):
        kp[b, core, part * 256:(part + 1) * 256, :] = smooth(core, part)

    def swap(r):
        return remote(kp.at[b, r], kp.at[b, r], kx_s.at[r], kx_r.at[r], pair)

    def z_copies(q):
        return [
            remote(zs.at[q], zr.at[q, i], z_s.at[q], z_r.at[q], dev)
            for i, dev in enumerate((zpart, zpair, pair))
        ]

    def z_all(q):
        return remote(zr.at[q], zr.at[q], z_s.at[q], z_r.at[q], sib)

    @pl.when(zh == 0)
    def _():
        pl.semaphore_wait(barrier, 2)

    own = []
    for q in batches:
        remote(r1.at[q, span], r1.at[q, span], rs_s.at[q], rs_r.at[q], sib).wait_recv()
        acc = r1[q, 0:n_cb, :].astype(F32)
        for s in range(1, n_xy):
            acc = acc + r1[q, s * n_cb:(s + 1) * n_cb, :].astype(F32)
        zs[q] = acc.astype(BF16)
        for cp in z_copies(q):
            cp.start()
        own.append(acc)

    swap(core).start()
    core_swap.wait_recv()

    @pl.when(zh == 0)
    def _():
        swap(other).start()

    for q, acc in zip(batches, own):
        z_all(q).wait_recv()

        def share(x):
            return jnp.where(b == 0, x[0:8, :], x[8:16, :])

        mine = share(acc + zr[q, 0].astype(F32))
        theirs = share(zr[q, 1].astype(F32) + zr[q, 2].astype(F32))
        even = jnp.where(b == 0, mine, theirs)
        odd = jnp.where(b == 0, theirs, mine)
        final = jnp.concatenate([even, odd], axis=0).astype(BF16)
        fc[q] = final

        def ag_start(i, c):
            _, dev = xy_dev(i)
            remote(
                fc.at[q], g.at[q, lanes, rows_of(cxy)], ag_s.at[q], ag_r.at[q], dev
            ).start()
            return c

        lax.fori_loop(0, n_xy - 1, ag_start, 0)
        g[q, lanes, rows_of(cxy), :] = final

    @pl.when(zh == 1)
    def _():
        swap(other).start()

    def forward(r, q):
        both = jnp.concatenate([g[q, 0], g[q, 1]], axis=1).astype(F32).reshape(16, 2, 8, 256)
        real = imag = 0.0
        for block in range(2):
            x = both[:, block].reshape(128, 256).astype(BF16)
            real = real + nt(x, kp[block, r, 0:256, :])
            imag = imag + nt(x, kp[block, r, 256:512, :])
        hr = (real[0:64, :] - imag[64:128, :]).astype(BF16)
        hi = (imag[0:64, :] + real[64:128, :]).astype(BF16)
        for aa in range(2):
            hs[q, r, aa, 0:pw, :] = hr[aa * pw:(aa + 1) * pw, :]
            hs[q, r, aa, pw:2 * pw, :] = hi[aa * pw:(aa + 1) * pw, :]

        @pl.when(q == half)
        def _():
            near(r).start()

        @pl.when((q != half) & (a == 1))
        def _():
            give(r).start()

    def near(r):
        return remote(
            hs.at[half, r, 1 - a], r2.at[core], h_s.at[r], h_r.at[core], (mate[0], col_of(r))
        )

    def far(r):
        return remote(
            hs.at[1 - half, r, 1], rd.at[core, a], fa_s.at[r], fa_r.at[core],
            ((1 - half) * n_j + 2 + b, col_of(r)),
        )

    def give(r):
        return remote(hs.at[1 - half, r, 0], rg.at[r], g_s.at[r], g_r.at[r], mate)

    def across(r):
        return remote(l2s.at[r], rc.at[core], cr_s.at[r], cr_r.at[core], (beyond[0], col_of(r)))

    def local():
        return remote(hs.at[half, other, a], rl, lo_s, lo_r, sib)

    def cross():
        for r in order_of_rows:
            give(r).wait_recv()
            l2s[r] = (hs[1 - half, r, 0].astype(F32) + rg[r].astype(F32)).astype(BF16)
            across(r).start()

    for q in batches:
        remote(r1.at[q, span], r1.at[q, span], ag_s.at[q], ag_r.at[q], sib).wait_recv()
        if q == 0:
            swap(core).wait_recv()
            swap(other).wait_recv()
        for r in order_of_rows:
            forward(r, q)

        @pl.when(q != half)
        def _():
            for r in order_of_rows:
                far(r).start()

        @pl.when(q == half)
        def _():
            local().start()

        @pl.when((q != half) & (a == 0))
        def _():
            cross()

    for f in (core, other):
        if f is core:
            total = hs[half, core, a].astype(F32)
        else:
            local().wait_recv()
            total = rl[...].astype(F32)
        remote(r2.at[f], r2.at[f], h_s.at[f], h_r.at[f], sib).wait_recv()
        total = total + r2[f].astype(F32)

        @pl.when(a == 0)
        def _():
            remote(rc.at[f], rc.at[f], cr_s.at[f], cr_r.at[f], sib).wait_recv()
            xs[...] = rc[f].astype(F32)

        @pl.when(a == 1)
        def _():
            remote(rd.at[f], rd.at[f], fa_s.at[f], fa_r.at[f], sib).wait_recv()
            xs[...] = rd[f, 0].astype(F32) + rd[f, 1].astype(F32)

        total = total + xs[...]
        level = nv_ref[pl.ds(f, 1), :]
        for c in range(2):
            first = pl.multiple_of(f * 512 + c * 256 + half * 128 + a * 64, 64)
            block = vv[pl.ds(first, 2 * pw), :].astype(F32).reshape(pw // 8, 2, 8, 256)
            mine = jnp.where(b == 0, block[:, 0], block[:, 1]).reshape(pw, 256)
            o_ref[pl.ds(pl.multiple_of((f * 2 + c) * pw, pw), pw), :] = (
                total[c * pw:(c + 1) * pw, :] + level * mine
            )

    @pl.when(row < n_row - 1)
    def _():
        for cp in up:
            cp.wait_send()

    @pl.when(row > 0)
    def _():
        for cp in down:
            cp.wait_send()

    for q in range(2):
        core_rs(q).wait_send()
        remote(r1.at[q, span], r1.at[q, span], rs_s.at[q], rs_r.at[q], sib).wait_send()
        z_all(q).wait_send()
        remote(r1.at[q, span], r1.at[q, span], ag_s.at[q], ag_r.at[q], sib).wait_send()
        swap(q).wait_send()
        near(q).wait_send()
        far(q).wait_send()

        @pl.when(a == 1)
        def _():
            give(q).wait_send()

        @pl.when(a == 0)
        def _():
            across(q).wait_send()

    core_swap.wait_send()
    local().wait_send()


def shards(kernel, probes, noise_var, prior_diag):
    n_row = lax.axis_size("row")
    n_col = lax.axis_size("col")
    n_j = n_row // 2
    pw = 256 // n_row
    n_cb = 512 // (n_col // 4)
    k = kernel.reshape(1024, 256)
    vmem = pl.BlockSpec(memory_space=pltpu.VMEM)
    hbm = pl.BlockSpec(memory_space=pltpu.HBM)
    dma = pltpu.SemaphoreType.DMA
    out = pl.pallas_call(
        functools.partial(body, n_row, n_col),
        out_shape=jax.ShapeDtypeStruct((4 * pw, 256), F32),
        in_specs=[hbm, hbm, hbm, hbm],
        out_specs=vmem,
        scratch_shapes=[
            pltpu.VMEM((1024, 256), BF16),
            pltpu.VMEM((256, 2, 2, 256), BF16),
            pltpu.VMEM((1024, 256), BF16),
            pltpu.VMEM((2, 256), F32),
            pltpu.VMEM((1, 256), F32),
            pltpu.VMEM((1024, 256), BF16),
            pltpu.VMEM((2, 8, 128), F32),
            pltpu.VMEM((2, 8, 128), F32),
            pltpu.VMEM((512, 256), BF16),
            pltpu.VMEM((2, 2, 512, 256), BF16),
            pltpu.VMEM((2, 2, 256, 128), BF16),
            pltpu.VMEM((2, 2, 256, 128), BF16),
            pltpu.VMEM((2, 2, 256, 128), F32),
            pltpu.VMEM((2, 2, 256, 128), BF16),
            pltpu.VMEM((2, 512, 128), BF16),
            pltpu.VMEM((2, n_cb, 128), BF16),
            pltpu.VMEM((2, 3, n_cb, 128), BF16),
            pltpu.VMEM((2, n_cb, 128), BF16),
            pltpu.VMEM((2, 2, 256, 128), BF16),
            pltpu.VMEM((2, 2, n_j // 2, 2 * pw, 256), BF16),
            pltpu.VMEM((2, 2 * pw, 256), BF16),
            pltpu.VMEM((2, 2 * pw, 256), BF16),
            pltpu.VMEM((2, 2 * pw, 256), BF16),
            pltpu.VMEM((2, 2 * pw, 256), BF16),
            pltpu.VMEM((2, 2, 2 * pw, 256), BF16),
            pltpu.VMEM((2 * pw, 256), F32),
            pltpu.VMEM((2 * pw, 256), BF16),
            dma((4,)), dma((4,)), dma((4,)), dma((2,)), dma((2,)), dma((2,)), dma((2,)), dma((2,)),
            dma((2,)), dma((2,)), dma((2,)), dma, dma,
            dma((2,)), dma((2,)), dma((2,)), dma((2,)), dma((2,)), dma((2,)), dma((2,)), dma((2,)),
            dma((2,)), dma((2,)), dma, dma,
        ],
        compiler_params=pltpu.CompilerParams(
            collective_id=0, has_side_effects=True, vmem_limit_bytes=60 * 1024 * 1024
        ),
    )(k, probes, noise_var, prior_diag.reshape(1, 256))
    return jnp.transpose(out.reshape(2, 2, pw, 256), (2, 0, 1, 3))


def solution(mesh):
    in_specs = (P(None, None, "col", "row"), P(None, None, None, "col"), P(None, "col"), P("row"))
    out_specs = P("row", None, None, "col")
    return jax.shard_map(shards, mesh=mesh, in_specs=in_specs, out_specs=out_specs, check_vma=False)
```

```python
import functools

import jax
import jax.numpy as jnp
from jax import lax
from jax.experimental import pallas as pl
from jax.experimental.pallas import tpu as pltpu
from jax.sharding import PartitionSpec as P

F32 = jnp.float32
BF16 = jnp.bfloat16
MESH = pl.DeviceIdType.MESH


def nt(a, b):
    return lax.dot_general(a, b, (((1,), (1,)), ((), ())), preferred_element_type=F32)


def nn(a, b):
    return jnp.dot(a, b, preferred_element_type=F32)


def body(
    n_row, n_col,
    k_hbm, v_hbm, nv_hbm, d_hbm, o_ref,
    kv, vraw, vv, nv_ref, d_ref, kh, dsend, dh, ks, kp, s0, r0, ao, s1, r1, zs, zr, fc, g, hs, r2, rg, l2s, rc, rl,
    load_sem, halo_s, halo_r, core_s, core_r, rs_s, rs_r, z_s, z_r, ag_s, ag_r, kc_s, kc_r,
    kx_s, kx_r, h_s, h_r, g_s, g_r, cr_s, cr_r, lo_s, lo_r,
):
    row = lax.axis_index("row")
    col = lax.axis_index("col")
    n_xy = n_col // 4
    n_j = n_row // 2
    core = lax.rem(col, 2)
    zh = lax.rem(lax.div(col, 2), 2)
    cxy = lax.div(col, 4)
    half = lax.div(row, n_j)
    j = lax.rem(row, n_j)
    a = lax.div(j, 2)
    b = lax.rem(j, 2)
    n_cb = 512 // n_xy
    pw = 256 // n_row
    other = 1 - core
    batches = (0, 1)

    sib = (row, cxy * 4 + zh * 2 + other)
    pair_row = row + 1 - 2 * b
    pair = (pair_row, col)
    zcol = cxy * 4 + (1 - zh) * 2 + core
    zpart = (row, zcol)
    zpair = (pair_row, zcol)
    mate = (half * n_j + (1 - a) * 2 + b, col)
    beyond = ((1 - half) * n_j + j, col)

    def col_of(r):
        return cxy * 4 + zh * 2 + r

    def xy_dev(i):
        step = lax.div(i + 1, 2)
        k = n_xy // 2 + jnp.where(lax.rem(i, 2) == 1, -step, step)
        t = lax.rem(cxy + k, n_xy)
        return t, (row, t * 4 + zh * 2 + core)

    def remote(src, dst, ss, rs, dev):
        return pltpu.make_async_remote_copy(
            src_ref=src, dst_ref=dst, send_sem=ss, recv_sem=rs, device_id=dev, device_id_type=MESH
        )

    barrier = pltpu.get_barrier_semaphore()

    def signal(dev):
        pl.semaphore_signal(barrier, inc=1, device_id=dev, device_id_type=MESH)

    def sig_xy(i, c):
        signal(xy_dev(i)[1])
        return c

    lax.fori_loop(0, n_xy - 1, sig_xy, 0)
    signal(beyond)
    signal(mate)
    signal((beyond[0], col_of(other)))
    signal((mate[0], col_of(other)))
    signal(pair)
    signal(sib)
    inland = (row > 0) & (row < n_row - 1)

    @pl.when(inland)
    def _():
        signal((row - 1 + 2 * b, col))

    loads = [
        pltpu.make_async_copy(src, dst, load_sem.at[i])
        for i, (src, dst) in enumerate(
            ((v_hbm, vraw), (k_hbm, kv), (d_hbm, d_ref), (nv_hbm, nv_ref))
        )
    ]
    for cp in loads:
        cp.start()

    loads[0].wait()

    def order(i, c):
        for f in range(2):
            x = jnp.swapaxes(vraw[pl.ds(i * 2 * pw, 2 * pw), f].astype(F32), 0, 1)
            x = jnp.swapaxes(x.reshape(2, 2, pw // 8, 8, 256), 1, 2).reshape(2, 2 * pw, 256)
            for part in range(2):
                first = pl.multiple_of((f * 2 + part) * 256 + i * 2 * pw, 2 * pw)
                vv[pl.ds(first, 2 * pw), :] = x[part].astype(BF16)
        return c

    lax.fori_loop(0, n_j, order, 0)
    loads[1].wait()

    def adjoint(f):
        base = pl.multiple_of(f * 512, 512)
        vr = vv[pl.ds(base, 256), :]
        vi = vv[pl.ds(base + 256, 256), :]
        kr = kv[pl.ds(base, 256), :]
        ki = kv[pl.ds(base + 256, 256), :]
        return nn(vr, kr) + nn(vi, ki), nn(vi, kr) - nn(vr, ki)

    def put(ref, parts):
        for c in range(2):
            for q in range(2):
                for h in range(2):
                    ref[q, h, c * 128:(c + 1) * 128, :] = parts[c][
                        q * 128:(q + 1) * 128, h * 128:(h + 1) * 128
                    ].astype(ref.dtype)

    put(s0, adjoint(other))
    met = n_xy - 1 + 6 + jnp.where(inland, 1, 0)
    pl.semaphore_wait(barrier, met + 2 * zh)
    signal(zpart)
    signal(zpair)

    def core_rs(q):
        return remote(s0.at[q], r0.at[q], core_s.at[q], core_r.at[q], sib)

    for q in batches:
        core_rs(q).start()
    loads[2].wait()
    loads[3].wait()
    dsend[0] = jnp.broadcast_to(d_ref[:, 128:256], (8, 128))
    dsend[1] = jnp.broadcast_to(d_ref[:, 0:128], (8, 128))
    up_dev = (jnp.minimum(row + 1, n_row - 1), col)
    down_dev = (jnp.maximum(row - 1, 0), col)
    up = [
        remote(kv.at[:, pl.ds(128, 128)], kh.at[:, pl.ds(0, 128)], halo_s.at[0], halo_r.at[0], up_dev),
        remote(dsend.at[0], dh.at[0], halo_s.at[1], halo_r.at[1], up_dev),
    ]
    down = [
        remote(kv.at[:, pl.ds(0, 128)], kh.at[:, pl.ds(128, 128)], halo_s.at[2], halo_r.at[2], down_dev),
        remote(dsend.at[1], dh.at[1], halo_s.at[3], halo_r.at[3], down_dev),
    ]

    @pl.when(row < n_row - 1)
    def _():
        for cp in up:
            cp.start()

    @pl.when(row > 0)
    def _():
        for cp in down:
            cp.start()

    put(ao, adjoint(core))

    def rows_of(t):
        return pl.ds(pl.multiple_of(lax.div(t, 2) * n_cb, n_cb), n_cb)

    slot = pl.ds(pl.multiple_of(cxy * n_cb, n_cb), n_cb)
    span = pl.ds(0, (n_xy - 1) * n_cb)
    lanes = lax.rem(cxy, 2)

    for q in batches:
        core_rs(q).wait_recv()
        s1[q] = (ao[q] + r0[q].astype(F32)).astype(BF16)

        def rs_start(i, c):
            t, dev = xy_dev(i)
            remote(
                s1.at[q, lax.rem(t, 2), rows_of(t)], r1.at[q, slot], rs_s.at[q], rs_r.at[q], dev
            ).start()
            return c

        lax.fori_loop(0, n_xy - 1, rs_start, 0)
        r1[q, slot, :] = s1[q, lanes, rows_of(cxy), :]

    @pl.when(row > 0)
    def _():
        for cp in up:
            cp.wait_recv()

    @pl.when(row < n_row - 1)
    def _():
        for cp in down:
            cp.wait_recv()

    @pl.when(row == 0)
    def _():
        kh[:, 0:128] = jnp.zeros((1024, 128), BF16)
        dh[0] = jnp.zeros((8, 128), F32)

    @pl.when(row == n_row - 1)
    def _():
        kh[:, 128:256] = jnp.zeros((1024, 128), BF16)
        dh[1] = jnp.zeros((8, 128), F32)

    lane = lax.broadcasted_iota(jnp.int32, (256, 256), 1)
    depth = lax.broadcasted_iota(jnp.int32, (256, 256), 0)
    d = d_ref[...]
    before = jnp.concatenate([dh[0, 0:1, :], d, dh[1, 0:1, :]], axis=1)
    left = pltpu.roll(before, 1, 1)[:, 128:384]
    right = pltpu.roll(before, 511, 1)[:, 128:384]
    ends = (lane == 0) & (row == 0) | (lane == 255) & (row == n_row - 1)

    def banded(gap):
        m = jnp.where(gap == 0, d * d + jnp.where(ends, 1.0, 2.0), 0.0)
        m = jnp.where(gap == -1, -(left + d), m)
        m = jnp.where(gap == 1, -(right + d), m)
        return jnp.where((gap == 2) | (gap == -2), 1.0, m)

    def thirds(m):
        a = m.astype(BF16)
        rest = m - a.astype(F32)
        b = rest.astype(BF16)
        return a, b, (rest - b.astype(F32)).astype(BF16)

    inner = thirds(banded(depth - lane))
    outer = thirds(banded(jnp.where(depth < 128, depth - 128, depth + 128) - lane))

    def smooth(f, part):
        rows = pl.ds(pl.multiple_of(f * 512 + part * 256, 256), 256)
        e = kv[rows, :]
        h = kh[rows, :]
        total = nn(e, inner[0]) + nn(h, outer[0])
        total = total + (nn(e, inner[1]) + nn(h, outer[1]))
        total = total + (nn(e, inner[2]) + nn(h, outer[2]))
        return total.astype(BF16)

    core_swap = remote(ks, kp.at[b, core], kc_s, kc_r, sib)
    for part in range(2):
        ks[part * 256:(part + 1) * 256, :] = smooth(other, part)
    core_swap.start()
    for part in range(2):
        kp[b, core, part * 256:(part + 1) * 256, :] = smooth(core, part)

    def swap(r):
        return remote(kp.at[b, r], kp.at[b, r], kx_s.at[r], kx_r.at[r], pair)

    def z_copies(q):
        return [
            remote(zs.at[q], zr.at[q, i], z_s.at[q], z_r.at[q], dev)
            for i, dev in enumerate((zpart, zpair, pair))
        ]

    def z_all(q):
        return remote(zr.at[q], zr.at[q], z_s.at[q], z_r.at[q], sib)

    @pl.when(zh == 0)
    def _():
        pl.semaphore_wait(barrier, 2)

    own = []
    for q in batches:
        remote(r1.at[q, span], r1.at[q, span], rs_s.at[q], rs_r.at[q], sib).wait_recv()
        acc = r1[q, 0:n_cb, :].astype(F32)
        for s in range(1, n_xy):
            acc = acc + r1[q, s * n_cb:(s + 1) * n_cb, :].astype(F32)
        zs[q] = acc.astype(BF16)
        for cp in z_copies(q):
            cp.start()
        own.append(acc)

    swap(core).start()
    core_swap.wait_recv()

    @pl.when(zh == 0)
    def _():
        swap(other).start()

    for q, acc in zip(batches, own):
        z_all(q).wait_recv()

        def share(x):
            return jnp.where(b == 0, x[0:8, :], x[8:16, :])

        mine = share(acc + zr[q, 0].astype(F32))
        theirs = share(zr[q, 1].astype(F32) + zr[q, 2].astype(F32))
        even = jnp.where(b == 0, mine, theirs)
        odd = jnp.where(b == 0, theirs, mine)
        final = jnp.concatenate([even, odd], axis=0).astype(BF16)
        fc[q] = final

        def ag_start(i, c):
            _, dev = xy_dev(i)
            remote(
                fc.at[q], g.at[q, lanes, rows_of(cxy)], ag_s.at[q], ag_r.at[q], dev
            ).start()
            return c

        lax.fori_loop(0, n_xy - 1, ag_start, 0)
        g[q, lanes, rows_of(cxy), :] = final

    @pl.when(zh == 1)
    def _():
        swap(other).start()

    def forward(r, q):
        both = jnp.concatenate([g[q, 0], g[q, 1]], axis=1).astype(F32).reshape(16, 2, 8, 256)
        real = imag = 0.0
        for block in range(2):
            x = both[:, block].reshape(128, 256).astype(BF16)
            real = real + nt(x, kp[block, r, 0:256, :])
            imag = imag + nt(x, kp[block, r, 256:512, :])
        hr = (real[0:64, :] - imag[64:128, :]).astype(BF16)
        hi = (imag[0:64, :] + real[64:128, :]).astype(BF16)
        for aa in range(2):
            hs[q, r, aa, 0:pw, :] = hr[aa * pw:(aa + 1) * pw, :]
            hs[q, r, aa, pw:2 * pw, :] = hi[aa * pw:(aa + 1) * pw, :]

        @pl.when(q == half)
        def _():
            near(r).start()

        @pl.when((q != half) & (a == 1))
        def _():
            give(r).start()

    def near(r):
        return remote(
            hs.at[half, r, 1 - a], r2.at[core], h_s.at[r], h_r.at[core], (mate[0], col_of(r))
        )

    def give(r):
        return remote(hs.at[1 - half, r, 1 - a], rg.at[r], g_s.at[r], g_r.at[r], mate)

    def across(r):
        return remote(l2s.at[r], rc.at[core], cr_s.at[r], cr_r.at[core], (beyond[0], col_of(r)))

    def local():
        return remote(hs.at[half, other, a], rl, lo_s, lo_r, sib)

    def cross(giving):
        for r in (core, other):
            give(r).wait_recv()
            l2s[r] = (hs[1 - half, r, a].astype(F32) + rg[r].astype(F32)).astype(BF16)
            across(r).start()
            if giving:
                give(r).start()

    for q in batches:
        remote(r1.at[q, span], r1.at[q, span], ag_s.at[q], ag_r.at[q], sib).wait_recv()
        if q == 0:
            swap(core).wait_recv()
        forward(core, q)
        if q == 0:
            swap(other).wait_recv()
        forward(other, q)

        @pl.when(q == half)
        def _():
            local().start()

        @pl.when((q != half) & (a == 0))
        def _():
            cross(True)

    @pl.when(a == 1)
    def _():
        cross(False)

    for f in (core, other):
        if f is core:
            total = hs[half, core, a].astype(F32)
        else:
            local().wait_recv()
            total = rl[...].astype(F32)
        remote(r2.at[f], r2.at[f], h_s.at[f], h_r.at[f], sib).wait_recv()
        total = total + r2[f].astype(F32)
        remote(rc.at[f], rc.at[f], cr_s.at[f], cr_r.at[f], sib).wait_recv()
        total = total + rc[f].astype(F32)
        level = nv_ref[pl.ds(f, 1), :]
        for c in range(2):
            first = pl.multiple_of(f * 512 + c * 256 + half * 128 + a * 64, 64)
            block = vv[pl.ds(first, 2 * pw), :].astype(F32).reshape(pw // 8, 2, 8, 256)
            mine = jnp.where(b == 0, block[:, 0], block[:, 1]).reshape(pw, 256)
            o_ref[pl.ds(pl.multiple_of((f * 2 + c) * pw, pw), pw), :] = (
                total[c * pw:(c + 1) * pw, :] + level * mine
            )

    @pl.when(row < n_row - 1)
    def _():
        for cp in up:
            cp.wait_send()

    @pl.when(row > 0)
    def _():
        for cp in down:
            cp.wait_send()

    for q in range(2):
        core_rs(q).wait_send()
        remote(r1.at[q, span], r1.at[q, span], rs_s.at[q], rs_r.at[q], sib).wait_send()
        z_all(q).wait_send()
        remote(r1.at[q, span], r1.at[q, span], ag_s.at[q], ag_r.at[q], sib).wait_send()
        swap(q).wait_send()
        near(q).wait_send()
        give(q).wait_send()
        across(q).wait_send()
    core_swap.wait_send()
    local().wait_send()


def shards(kernel, probes, noise_var, prior_diag):
    n_row = lax.axis_size("row")
    n_col = lax.axis_size("col")
    n_j = n_row // 2
    pw = 256 // n_row
    n_cb = 512 // (n_col // 4)
    k = kernel.reshape(1024, 256)
    vmem = pl.BlockSpec(memory_space=pltpu.VMEM)
    hbm = pl.BlockSpec(memory_space=pltpu.HBM)
    dma = pltpu.SemaphoreType.DMA
    out = pl.pallas_call(
        functools.partial(body, n_row, n_col),
        out_shape=jax.ShapeDtypeStruct((4 * pw, 256), F32),
        in_specs=[hbm, hbm, hbm, hbm],
        out_specs=vmem,
        scratch_shapes=[
            pltpu.VMEM((1024, 256), BF16),
            pltpu.VMEM((256, 2, 2, 256), BF16),
            pltpu.VMEM((1024, 256), BF16),
            pltpu.VMEM((2, 256), F32),
            pltpu.VMEM((1, 256), F32),
            pltpu.VMEM((1024, 256), BF16),
            pltpu.VMEM((2, 8, 128), F32),
            pltpu.VMEM((2, 8, 128), F32),
            pltpu.VMEM((512, 256), BF16),
            pltpu.VMEM((2, 2, 512, 256), BF16),
            pltpu.VMEM((2, 2, 256, 128), BF16),
            pltpu.VMEM((2, 2, 256, 128), BF16),
            pltpu.VMEM((2, 2, 256, 128), F32),
            pltpu.VMEM((2, 2, 256, 128), BF16),
            pltpu.VMEM((2, 512, 128), BF16),
            pltpu.VMEM((2, n_cb, 128), BF16),
            pltpu.VMEM((2, 3, n_cb, 128), BF16),
            pltpu.VMEM((2, n_cb, 128), BF16),
            pltpu.VMEM((2, 2, 256, 128), BF16),
            pltpu.VMEM((2, 2, n_j // 2, 2 * pw, 256), BF16),
            pltpu.VMEM((2, 2 * pw, 256), BF16),
            pltpu.VMEM((2, 2 * pw, 256), BF16),
            pltpu.VMEM((2, 2 * pw, 256), BF16),
            pltpu.VMEM((2, 2 * pw, 256), BF16),
            pltpu.VMEM((2 * pw, 256), BF16),
            dma((4,)), dma((4,)), dma((4,)), dma((2,)), dma((2,)), dma((2,)), dma((2,)), dma((2,)),
            dma((2,)), dma((2,)), dma((2,)), dma, dma,
            dma((2,)), dma((2,)), dma((2,)), dma((2,)), dma((2,)), dma((2,)), dma((2,)), dma((2,)),
            dma, dma,
        ],
        compiler_params=pltpu.CompilerParams(
            collective_id=0, has_side_effects=True, vmem_limit_bytes=60 * 1024 * 1024
        ),
    )(k, probes, noise_var, prior_diag.reshape(1, 256))
    return jnp.transpose(out.reshape(2, 2, pw, 256), (2, 0, 1, 3))


def solution(mesh):
    in_specs = (P(None, None, "col", "row"), P(None, None, None, "col"), P(None, "col"), P("row"))
    out_specs = P("row", None, None, "col")
    return jax.shard_map(shards, mesh=mesh, in_specs=in_specs, out_specs=out_specs, check_vma=False)
```
